32 devices in a mesh: wide: 8 (over y, x, core), oct: 4 (over z).
Axes of the slice: x: 2, y: 2, z: 4, core: 2. Of those that a mesh axis runs over, the one named last changes fastest.
Arguments:
- positions: float32 [3, 65536], P(None, ('wide', 'oct'))
- masses: float32 [65536], P(('wide', 'oct')), may hold values from 0.5 to 2
- counts: int32 [256], P(('wide', 'oct')), may hold values from 64 to 256, as said below
- near_list: int32 [256, 8], P(('wide', 'oct')), may hold values from 0 to 47, as said below
- far_list: int32 [256, 16], P(('wide', 'oct')), may hold values from 0 to 127, as said below
Outputs:
- acceleration: float32 [3, 65536], P(None, ('wide', 'oct'))
The draws below stay inside these ranges and needn't reach their ends.
Inputs may be any that keep to these rules, and one draw needn't show every extreme that they name: counts lie between 64 and 256; both ends are reached. `near_list`: on every device the lists of its blocks together name every level 0 to 5; two entries of one block never name the same block. `far_list`: on every device the lists of its blocks together name every wide level 0 to 3.
All inputs are finite; a program needn't handle non-finite values.
Results may differ from the reference program's by a relative error of at most 0.0003.
Values sent between devices are 32-bit elements; how exact they have to be, the bound alone decides.
A program may use at most 64 MiB of HBM per device.

```python
import math
import jax
import jax.numpy as jnp
from jax import lax

LEAF = 256
BLK_DEV = 8
NEAR = 8
FAR = 16
WIDE_BITS = 3
LEVELS = 5
BLOCKS = 256
BODIES = 65536
N_WIDE = 8
N_OCT = 4


def draw_positions(key, part):
    key_one, key_two = jax.random.split(key)
    centres = jax.random.uniform(key_one, (3, BLOCKS, 1), jnp.float32, -2.0, 2.0)
    offsets = jnp.clip(0.5 * jax.random.normal(key_two, (3, BLOCKS, LEAF), jnp.float32), -2.0, 2.0)
    return (centres + offsets).reshape(3, BODIES)


def draw_counts(key, part):
    key_one, key_two, key_three = jax.random.split(jax.random.fold_in(key, 11), 3)
    counts = jax.random.randint(key_one, (BLOCKS,), LEAF // 4, LEAF + 1)
    full_index = jax.random.randint(key_two, (), 0, BLOCKS)
    low_index = (full_index + 1 + jax.random.randint(key_three, (), 0, BLOCKS - 1)) % BLOCKS
    counts = counts.at[full_index].set(LEAF)
    counts = counts.at[low_index].set(LEAF // 4)
    return counts.astype(jnp.int32)


def device_levels(key, sets_count, entries):
    devices = N_WIDE * N_OCT
    keys_all = jax.random.split(key, devices)
    orders = jax.vmap(lambda single: jax.random.permutation(single, sets_count))(keys_all)
    block_index = jnp.arange(BLOCKS, dtype=jnp.int32)
    local = block_index % BLK_DEV
    entry_index = jnp.arange(entries, dtype=jnp.int32)
    position = (local[:, None] + entry_index[None, :]) % sets_count
    rows_order = orders[block_index // BLK_DEV]
    return jnp.take_along_axis(rows_order, position, axis=1).astype(jnp.int32)


def draw_near_list(key, part):
    key_one, key_two = jax.random.split(jax.random.fold_in(key, 23))
    sets_count = LEVELS + 1
    level_index = device_levels(key_one, sets_count, NEAR)
    base_slot = jax.random.randint(key_two, (BLOCKS, sets_count), 0, BLK_DEV)
    entry_index = jnp.arange(NEAR, dtype=jnp.int32)
    slot_index = (jnp.take_along_axis(base_slot, level_index, axis=1) + entry_index[None, :] // sets_count) % BLK_DEV
    return (level_index * BLK_DEV + slot_index).astype(jnp.int32)


def draw_far_list(key, part):
    key_one, key_two, key_three = jax.random.split(jax.random.fold_in(key, 37), 3)
    sets_count = WIDE_BITS + 1
    level_index = device_levels(key_one, sets_count, FAR)
    member = jax.random.randint(key_two, (BLOCKS, FAR), 0, N_OCT)
    slot_index = jax.random.randint(key_three, (BLOCKS, FAR), 0, BLK_DEV)
    return (level_index * (N_OCT * BLK_DEV) + member * BLK_DEV + slot_index).astype(jnp.int32)


def shard_levels(key, shape, shards, least, top_value):
    level = 1.0
    for axis_at, blocks in shards:
        draws = jax.random.uniform(jax.random.fold_in(jax.random.fold_in(key, 6), axis_at), (blocks,), jnp.float32, least / len(shards), top_value / len(shards))
        level = level * jnp.repeat(jnp.exp(draws), shape[axis_at] // blocks).reshape((-1,) + (1,) * (len(shape) - 1 - axis_at))
    return level


def setup_inputs(seed: int = 0) -> dict:
    key_list = jax.random.split(jax.random.key(seed), 6)
    return {
        "positions": draw_positions(jax.random.fold_in(key_list[5], 71), 0),
        "masses": jnp.clip(jnp.exp(math.log(2.0) - 1.3862944 * jax.random.uniform(key_list[1], (BODIES,), jnp.float32) ** shard_levels(key_list[1], (BODIES,), ((0, 32),), -0.2, 0.2)), 0.5, 2.0),
        "counts": draw_counts(jax.random.fold_in(key_list[5], 71), 0),
        "near_list": draw_near_list(jax.random.fold_in(key_list[5], 71), 0),
        "far_list": draw_far_list(jax.random.fold_in(key_list[5], 71), 0),
    }


near_soft = 0.01
far_soft = 0.25

def near_term(targets, sources, source_mass):
    delta = sources[:, :, None, :] - targets[:, :, :, None]
    dist_sq = lax.optimization_barrier(jnp.sum(delta * delta, axis=0)) + near_soft
    inverse = lax.rsqrt(dist_sq)
    weight = source_mass[:, None, :] * (inverse * inverse * inverse)
    return lax.optimization_barrier(jnp.sum(delta * weight[None], axis=3))

def cell_moments(block_pos, block_mass):
    total = lax.optimization_barrier(jnp.sum(block_mass, axis=1))
    centre = lax.optimization_barrier(jnp.sum(block_pos * block_mass[None], axis=2)) / total[None]
    offset = block_pos - centre[:, :, None]
    radius_sq = lax.optimization_barrier(jnp.sum(offset * offset, axis=0))
    trace_part = lax.optimization_barrier(jnp.sum(block_mass * radius_sq, axis=1))

    def second(first_axis, other_axis):
        return lax.optimization_barrier(jnp.sum(block_mass * 3.0 * offset[first_axis] * offset[other_axis], axis=1))
    return jnp.stack([total, centre[0], centre[1], centre[2], second(0, 0) - trace_part, second(1, 1) - trace_part, second(2, 2) - trace_part, second(0, 1), second(0, 2), second(1, 2)])

def far_term(targets, chosen):
    rel = targets[:, :, None, :] - chosen[1:4, :, :, None]
    dist_sq = lax.optimization_barrier(jnp.sum(rel * rel, axis=0)) + far_soft
    inverse = lax.rsqrt(dist_sq)
    inv_sq = inverse * inverse
    inv_three = inverse * inv_sq
    inv_five = inv_three * inv_sq
    inv_seven = inv_five * inv_sq
    quad = chosen[4:10][:, :, :, None]
    qr_x = quad[0] * rel[0] + quad[3] * rel[1] + quad[4] * rel[2]
    qr_y = quad[3] * rel[0] + quad[1] * rel[1] + quad[5] * rel[2]
    qr_z = quad[4] * rel[0] + quad[5] * rel[1] + quad[2] * rel[2]
    rqr = rel[0] * qr_x + rel[1] * qr_y + rel[2] * qr_z
    radial = -chosen[0][:, :, None] * inv_three - 2.5 * rqr * inv_seven
    accel = rel * radial[None] + jnp.stack([qr_x, qr_y, qr_z]) * inv_five[None]
    return lax.optimization_barrier(jnp.sum(accel, axis=2))

def level_flip(level_index):
    return jnp.where(level_index > 0, jnp.left_shift(jnp.int32(1), jnp.maximum(level_index - 1, 0)), 0).astype(jnp.int32)

def reference(positions, masses, counts, near_list, far_list):
    devices = N_WIDE * N_OCT
    grav = 1.0 / (NEAR * LEAF)
    valid_mask = (lax.broadcasted_iota(jnp.int32, (BLOCKS, LEAF), 1) < counts[:, None]).astype(jnp.float32)
    block_pos = positions.reshape(3, BLOCKS, LEAF)
    block_mass = masses.reshape(BLOCKS, LEAF) * valid_mask
    cells = cell_moments(block_pos, block_mass)
    group_cells = N_OCT * BLK_DEV

    def one_device(device):
        first = (device * BLK_DEV).astype(jnp.int32)
        targets = lax.dynamic_slice_in_dim(block_pos, first, BLK_DEV, 1)
        near_rows = lax.dynamic_slice_in_dim(near_list, first, BLK_DEV, 0)
        source_block = jnp.bitwise_xor(device, level_flip(near_rows // BLK_DEV)) * BLK_DEV + near_rows % BLK_DEV
        source_pos = block_pos[:, source_block]
        source_mass = block_mass[source_block]
        near_sum = jnp.zeros((3, BLK_DEV, LEAF), jnp.float32)
        for entry in range(NEAR):
            near_sum = near_sum + near_term(targets, source_pos[:, :, entry], source_mass[:, entry])
        far_rows = lax.dynamic_slice_in_dim(far_list, first, BLK_DEV, 0)
        remain = far_rows % group_cells
        wide_index = jnp.bitwise_xor(device // N_OCT, level_flip(far_rows // group_cells))
        cell_block = (wide_index * N_OCT + remain // BLK_DEV) * BLK_DEV + remain % BLK_DEV
        far_sum = far_term(targets, cells[:, cell_block])
        mask_dev = lax.dynamic_slice_in_dim(valid_mask, first, BLK_DEV, 0)
        return ((near_sum + far_sum) * grav * mask_dev[None]).reshape(3, BLK_DEV * LEAF)
    result = lax.map(one_device, jnp.arange(devices, dtype=jnp.int32))
    return jnp.transpose(result, (1, 0, 2)).reshape(3, BODIES)
```

```python
import functools

import jax
import jax.numpy as jnp
from jax import lax
from jax.experimental import pallas as pl
from jax.experimental.pallas import tpu as pltpu
from jax.sharding import PartitionSpec as P

NEAR_SOFT = 0.01
FAR_SOFT = 0.25
MESH = pl.DeviceIdType.MESH
TILE = 8
LANES = 128
CELL = 10
BF = jnp.bfloat16
F32 = jnp.float32
NT = (((1,), (1,)), ((), ()))


def split3(a):
    one = a.astype(BF).astype(F32)
    rest = a - one
    two = rest.astype(BF).astype(F32)
    return one, two, rest - two


def dot(a, b):
    return jnp.dot(a, b, preferred_element_type=F32)


def partners(wide, octs):
    flips = [0] + [1 << k for k in range(wide.bit_length() - 1)]
    return [(i, f, x) for i, f in enumerate(flips) for x in range(octs) if f or x]


def kernel(
    wide, octs, cnt_ref, near_ref, far_ref, pos_ref, mass_ref, out_ref,
    src, soa, feat, centre, cells, chosen, param, send_n, recv_n, send_c, recv_c,
):
    blocks, near = near_ref.shape
    far = far_ref.shape[1]
    leaf = pos_ref.shape[1] // blocks
    w, o = lax.axis_index("wide"), lax.axis_index("oct")
    reach = partners(wide, octs)
    barrier = pltpu.get_barrier_semaphore()
    for _, f, x in reach:
        pl.semaphore_signal(barrier, inc=1, device_id=(w ^ f, o ^ x), device_id_type=MESH)

    lane = lax.broadcasted_iota(jnp.int32, (1, leaf), 1)
    for b in range(blocks):
        cols = slice(b * leaf, (b + 1) * leaf)
        row = b % 2 * 4
        xyz = pos_ref[:, cols]
        live = jnp.where(lane < cnt_ref[b], mass_ref[:, cols], 0.0)
        src[0, b // 2, row : row + 3, :] = xyz
        src[0, b // 2, row + 3 : row + 4, :] = live
        for a in range(3):
            soa[a, b : b + 1, :] = xyz[a : a + 1]
        soa[3, b : b + 1, :] = live

    mass = soa[3]
    total = jnp.sum(mass, axis=1, keepdims=True)
    mid = [jnp.sum(mass * soa[a], axis=1, keepdims=True) / total for a in range(3)]
    off = [soa[a] - mid[a] for a in range(3)]
    radius_sq = off[0] * off[0] + off[1] * off[1] + off[2] * off[2]
    trace = jnp.sum(mass * radius_sq, axis=1, keepdims=True)

    def second(i, j):
        return jnp.sum(mass * 3.0 * off[i] * off[j], axis=1, keepdims=True)

    moments = [total] + mid
    moments += [second(a, a) - trace for a in range(3)]
    moments += [second(0, 1), second(0, 2), second(1, 2)]
    at = lax.broadcasted_iota(jnp.int32, (blocks, LANES), 1)
    held = jnp.zeros((blocks, LANES), F32)
    for k, moment in enumerate(moments):
        held = jnp.where(at // blocks == k, moment, held)
    held = jnp.where(at % blocks == lax.broadcasted_iota(jnp.int32, (blocks, LANES), 0), held, 0.0)
    cells[0] = jnp.sum(held, axis=0, keepdims=True)

    pl.semaphore_wait(barrier, len(reach))
    copies = []
    flips = [(0, 1 << k) for k in range(octs.bit_length() - 1)]
    flips += [(1 << k, 0) for k in range(wide.bit_length() - 1)]
    for k, (f, x) in enumerate(flips):
        copies.append(pltpu.make_async_remote_copy(
            src_ref=src.at[0], dst_ref=src.at[k + 1], send_sem=send_n.at[k], recv_sem=recv_n.at[k],
            device_id=(w ^ f, o ^ x), device_id_type=MESH,
        ))
    for k, (i, f, x) in enumerate(reach):
        copies.append(pltpu.make_async_remote_copy(
            src_ref=cells.at[0], dst_ref=cells.at[i * octs + x], send_sem=send_c.at[k], recv_sem=recv_c.at[k],
            device_id=(w ^ f, o ^ x), device_id_type=MESH,
        ))
    for copy in copies:
        copy.start()

    sub = lax.broadcasted_iota(jnp.int32, (TILE, leaf), 0)
    for b in range(blocks):
        c = [jnp.broadcast_to(mid[a][b : b + 1], (1, leaf)) for a in range(3)]
        rows = jnp.where(sub == 0, c[0], jnp.where(sub == 1, c[1], jnp.where(sub == 2, c[2], 0.0)))
        centre[b] = rows
        p = [off[a][b : b + 1] for a in range(3)]
        norm = radius_sq[b : b + 1] + NEAR_SOFT
        t = jnp.where(sub == 0, p[0], jnp.where(sub == 1, p[1], p[2])) * -2.0
        t = jnp.where(sub < 3, t, jnp.where(sub == 3, 1.0, jnp.where(sub == 4, norm, 0.0)))
        t1, t2, t3 = split3(t)
        stack = jnp.concatenate([t1, t2, t3, t1, t2, t1], axis=0)
        feat[b] = stack.T.astype(BF)

    for copy in copies:
        copy.wait()

    slot_at = lax.broadcasted_iota(jnp.int32, (1, LANES), 1) % blocks

    def choose(b, carry):
        for v in range(far):
            name = far_ref[b, v]
            rest = name % (octs * blocks)
            which = name // (octs * blocks) * octs + ((rest // blocks) ^ o)
            chosen[b, v : v + 1, :] = jnp.where(slot_at == rest % blocks, cells[which], 0.0)
        return carry

    lax.fori_loop(0, blocks, choose, 0)
    spread = (
        lax.broadcasted_iota(jnp.int32, (LANES, LANES), 0) // blocks
        == lax.broadcasted_iota(jnp.int32, (LANES, LANES), 1)
    ).astype(F32).astype(BF)
    picked = [part.astype(BF) for part in split3(chosen[...].reshape(blocks * far, LANES))]
    param[...] = (dot(picked[0], spread) + dot(picked[1], spread) + dot(picked[2], spread)).reshape(
        blocks, far, LANES
    )

    scale = 1.0 / (near * leaf)

    def target(b, carry):
        mid_b = centre[b]
        grid = feat[b]
        acc = jnp.zeros((4 * TILE, leaf), F32)
        for v in range(near):
            name = near_ref[b, v]
            slot = name % blocks
            raw = src[name // blocks, slot // 2]
            raw = jnp.where(slot % 2 == 1, pltpu.roll(raw, 4, 0), raw)
            m = raw[3:4]
            q = jnp.where(sub < 3, raw - mid_b, 0.0)
            norm = jnp.sum(q * q, axis=0, keepdims=True)
            s = jnp.where(sub < 3, q, jnp.where(sub == 3, norm, jnp.where(sub == 4, 1.0, 0.0)))
            s1, s2, s3 = split3(s)
            stack = jnp.concatenate([s1, s1, s1, s2, s2, s3], axis=0).astype(BF)
            a1, a2, a3 = split3(jnp.where(sub < 3, q, jnp.where(sub == 3, 1.0, 0.0)) * m)
            amount = jnp.concatenate([a1, a2, a3, jnp.zeros_like(a1)], axis=0).astype(BF)
            dist_sq = jnp.maximum(dot(grid, stack), NEAR_SOFT)
            inverse = lax.rsqrt(dist_sq)
            weight = inverse * inverse * inverse
            high = weight.astype(BF)
            low = (weight - high.astype(F32)).astype(BF)
            acc += lax.dot_general(amount, high, NT, preferred_element_type=F32)
            acc += lax.dot_general(amount, low, NT, preferred_element_type=F32)
        acc = acc[:TILE] + acc[TILE : 2 * TILE] + acc[2 * TILE : 3 * TILE]
        pair = src[0, b // 2]
        own = jnp.where(b % 2 == 1, pltpu.roll(pair, 4, 0), pair)
        near_sum = acc[:3] - (own - mid_b)[:3] * acc[3:4]

        par = param[b]
        col = [par[:, k : k + 1] for k in range(CELL)]
        rel = [own[a : a + 1] - col[1 + a] for a in range(3)]
        dist_sq = rel[0] * rel[0] + rel[1] * rel[1] + rel[2] * rel[2] + FAR_SOFT
        inverse = lax.rsqrt(dist_sq)
        inv_sq = inverse * inverse
        inv_three = inverse * inv_sq
        inv_five = inv_three * inv_sq
        inv_seven = inv_five * inv_sq
        xx, yy, zz, xy, xz, yz = col[4:]
        qr = [
            xx * rel[0] + xy * rel[1] + xz * rel[2],
            xy * rel[0] + yy * rel[1] + yz * rel[2],
            xz * rel[0] + yz * rel[1] + zz * rel[2],
        ]
        rqr = rel[0] * qr[0] + rel[1] * qr[1] + rel[2] * qr[2]
        radial = -col[0] * inv_three - 2.5 * rqr * inv_seven
        live = lane < cnt_ref[b]
        for a in range(3):
            far_sum = jnp.sum(rel[a] * radial + qr[a] * inv_five, axis=0, keepdims=True)
            result = jnp.where(live, (near_sum[a : a + 1] + far_sum) * scale, 0.0)
            out_ref[a : a + 1, pl.ds(pl.multiple_of(b * leaf, leaf), leaf)] = result
        return carry

    lax.fori_loop(0, blocks, target, 0)


def solution(mesh):
    wide, octs = mesh.shape["wide"], mesh.shape["oct"]

    def on_device(positions, masses, counts, near_list, far_list):
        blocks, near = near_list.shape
        far = far_list.shape[1]
        bodies = positions.shape[1]
        leaf = bodies // blocks
        steps = octs.bit_length() + wide.bit_length() - 2
        reach = len(partners(wide, octs))
        return pl.pallas_call(
            functools.partial(kernel, wide, octs),
            out_shape=jax.ShapeDtypeStruct((3, bodies), F32),
            in_specs=[pl.BlockSpec(memory_space=pltpu.SMEM)] * 3
            + [pl.BlockSpec(memory_space=pltpu.VMEM)] * 2,
            out_specs=pl.BlockSpec(memory_space=pltpu.VMEM),
            scratch_shapes=[
                pltpu.VMEM((steps + 1, blocks // 2, TILE, leaf), F32),
                pltpu.VMEM((4, blocks, leaf), F32),
                pltpu.VMEM((blocks, leaf, 6 * TILE), BF),
                pltpu.VMEM((blocks, TILE, leaf), F32),
                pltpu.VMEM((reach + 1, 1, LANES), F32),
                pltpu.VMEM((blocks, far, LANES), F32),
                pltpu.VMEM((blocks, far, LANES), F32),
                pltpu.SemaphoreType.DMA((steps,)),
                pltpu.SemaphoreType.DMA((steps,)),
                pltpu.SemaphoreType.DMA((reach,)),
                pltpu.SemaphoreType.DMA((reach,)),
            ],
            compiler_params=pltpu.CompilerParams(
                collective_id=0, has_side_effects=True, vmem_limit_bytes=32 * 1024 * 1024
            ),
        )(counts, near_list, far_list, positions, masses.reshape(1, bodies))

    return jax.shard_map(
        on_device,
        mesh=mesh,
        in_specs=(
            P(None, ("wide", "oct")),
            P(("wide", "oct")),
            P(("wide", "oct")),
            P(("wide", "oct"), None),
            P(("wide", "oct"), None),
        ),
        out_specs=P(None, ("wide", "oct")),
        check_vma=False,
    )
```

```python
import functools

import jax
import jax.numpy as jnp
from jax import lax
from jax.experimental import pallas as pl
from jax.experimental.pallas import tpu as pltpu
from jax.sharding import PartitionSpec as P

NEAR_SOFT = 0.01
FAR_SOFT = 0.25
MESH = pl.DeviceIdType.MESH
TILE = 8
LANES = 128
CELL = 10
BF = jnp.bfloat16
F32 = jnp.float32
NT = (((1,), (1,)), ((), ()))


def split3(a):
    one = a.astype(BF).astype(F32)
    rest = a - one
    two = rest.astype(BF).astype(F32)
    return one, two, rest - two


def dot(a, b):
    return jnp.dot(a, b, preferred_element_type=F32)


def kernel(
    wide, octs, cnt_in, near_in, far_in, pos_in, mass_in, out_ref,
    cnt_ref, near_ref, far_ref, pos_ref, mass_ref,
    src, soa, feat, centre, cells, picks, slots, fields, load, send_n, recv_n, send_c, recv_c, send_r, recv_r,
):
    blocks, near = near_ref.shape
    far = far_ref.shape[1]
    leaf = pos_ref.shape[1] // blocks
    w, o = lax.axis_index("wide"), lax.axis_index("oct")
    flips = [(0, 1 << k) for k in range(octs.bit_length() - 1)]
    flips += [(1 << k, 0) for k in range(wide.bit_length() - 1)]
    sets = wide.bit_length()
    barrier = pltpu.get_barrier_semaphore()
    for f, x in flips:
        pl.semaphore_signal(barrier, inc=1, device_id=(w ^ f, o ^ x), device_id_type=MESH)

    taken = [
        pltpu.make_async_copy(a, b, load.at[k])
        for k, (a, b) in enumerate([
            (pos_in, pos_ref), (mass_in, mass_ref), (cnt_in, cnt_ref), (near_in, near_ref), (far_in, far_ref),
        ])
    ]
    for copy in taken:
        copy.start()
    for copy in taken[:3]:
        copy.wait()

    lane = lax.broadcasted_iota(jnp.int32, (1, leaf), 1)
    for b in range(blocks):
        cols = slice(b * leaf, (b + 1) * leaf)
        row = b % 2 * 4
        xyz = pos_ref[:, cols]
        live = jnp.where(lane < cnt_ref[b], mass_ref[:, cols], 0.0)
        src[0, b // 2, row : row + 3, :] = xyz
        src[0, b // 2, row + 3 : row + 4, :] = live
        for a in range(3):
            soa[a, b : b + 1, :] = xyz[a : a + 1]
        soa[3, b : b + 1, :] = live

    pl.semaphore_wait(barrier, len(flips))
    copies = []
    for k, (f, x) in enumerate(flips):
        copies.append(pltpu.make_async_remote_copy(
            src_ref=src.at[0], dst_ref=src.at[k + 1], send_sem=send_n.at[k], recv_sem=recv_n.at[k],
            device_id=(w ^ f, o ^ x), device_id_type=MESH,
        ))
    for copy in copies:
        copy.start()

    mass = soa[3]
    total = jnp.sum(mass, axis=1, keepdims=True)
    mid = [jnp.sum(mass * soa[a], axis=1, keepdims=True) / total for a in range(3)]
    off = [soa[a] - mid[a] for a in range(3)]
    radius_sq = off[0] * off[0] + off[1] * off[1] + off[2] * off[2]
    trace = jnp.sum(mass * radius_sq, axis=1, keepdims=True)

    def second(i, j):
        return jnp.sum(mass * 3.0 * off[i] * off[j], axis=1, keepdims=True)

    moments = [total] + mid
    moments += [second(a, a) - trace for a in range(3)]
    moments += [second(0, 1), second(0, 2), second(1, 2)]
    at = lax.broadcasted_iota(jnp.int32, (blocks, LANES), 1)
    held = jnp.zeros((blocks, LANES), F32)
    for k, moment in enumerate(moments):
        held = jnp.where(at // blocks == k, moment, held)
    held = jnp.where(at % blocks == lax.broadcasted_iota(jnp.int32, (blocks, LANES), 0), held, 0.0)
    cells[0] = jnp.sum(held, axis=0, keepdims=True)

    for k in range(sets - 1):
        copies.append(pltpu.make_async_remote_copy(
            src_ref=cells.at[0], dst_ref=cells.at[k + 1], send_sem=send_c.at[k], recv_sem=recv_c.at[k],
            device_id=(w ^ 1 << k, o), device_id_type=MESH,
        ))
    for copy in copies[len(flips) :]:
        copy.start()

    for copy in taken[3:]:
        copy.wait()
    lane_at = lax.broadcasted_iota(jnp.int32, (1, LANES), 1)
    set_at = lax.broadcasted_iota(jnp.int32, (1, sets * octs), 1)

    def name_cells(b, carry):
        for v in range(far):
            name = far_ref[b, v]
            rest = name % (octs * blocks)
            which = ((rest // blocks) ^ o) * sets + name // (octs * blocks)
            picks[b, v : v + 1, :] = jnp.where(set_at == which, 1.0, 0.0)
            slots[b, v : v + 1, :] = jnp.where(lane_at % blocks == rest % blocks, 1.0, 0.0)
        return carry

    lax.fori_loop(0, blocks, name_cells, 0)

    sub = lax.broadcasted_iota(jnp.int32, (TILE, leaf), 0)
    for b in range(blocks):
        c = [jnp.broadcast_to(mid[a][b : b + 1], (1, leaf)) for a in range(3)]
        rows = jnp.where(sub == 0, c[0], jnp.where(sub == 1, c[1], jnp.where(sub == 2, c[2], 0.0)))
        centre[b] = rows
        p = [off[a][b : b + 1] for a in range(3)]
        norm = radius_sq[b : b + 1] + NEAR_SOFT
        t = jnp.where(sub == 0, p[0], jnp.where(sub == 1, p[1], p[2])) * -2.0
        t = jnp.where(sub < 3, t, jnp.where(sub == 3, 1.0, jnp.where(sub == 4, norm, 0.0)))
        t1, t2, t3 = split3(t)
        stack = jnp.concatenate([t1, t2, t3, t1, t2, t1], axis=0)
        feat[b] = stack.astype(BF)

    for copy in copies:
        copy.wait()

    def near_field(b, carry):
        mid_b = centre[b]
        grid = feat[b]
        acc = jnp.zeros((4 * TILE, leaf), F32)
        for v in range(near):
            name = near_ref[b, v]
            slot = name % blocks
            raw = src[name // blocks, slot // 2]
            raw = jnp.where(slot % 2 == 1, pltpu.roll(raw, 4, 0), raw)
            m = raw[3:4]
            q = jnp.where(sub < 3, raw - mid_b, 0.0)
            norm = jnp.sum(q * q, axis=0, keepdims=True)
            s = jnp.where(sub < 3, q, jnp.where(sub == 3, norm, jnp.where(sub == 4, 1.0, 0.0)))
            s1, s2, s3 = split3(s)
            stack = jnp.concatenate([s1, s1, s1, s2, s2, s3], axis=0).astype(BF)
            a1, a2, a3 = split3(jnp.where(sub < 3, q, jnp.where(sub == 3, 1.0, 0.0)) * m)
            amount = jnp.concatenate([a1, a2, a3, jnp.zeros_like(a1)], axis=0).astype(BF)
            dist_sq = jnp.maximum(lax.dot_general(stack, grid, (((0,),(0,)),((),())), preferred_element_type=F32), NEAR_SOFT)
            inverse = lax.rsqrt(dist_sq)
            weight = inverse * inverse * inverse
            high = weight.astype(BF)
            low = (weight - high.astype(F32)).astype(BF)
            acc += dot(amount, high)
            acc += dot(amount, low)
        acc = acc[:TILE] + acc[TILE : 2 * TILE] + acc[2 * TILE : 3 * TILE]
        pair = src[0, b // 2]
        own = jnp.where(b % 2 == 1, pltpu.roll(pair, 4, 0), pair)
        fields[b, :3, :] = acc[:3] - (own - mid_b)[:3] * acc[3:4]
        return carry

    steps = octs.bit_length() - 1
    for k in range(steps):
        count = sets << k
        relay = pltpu.make_async_remote_copy(
            src_ref=cells.at[pl.ds(0, count)], dst_ref=cells.at[pl.ds(count, count)],
            send_sem=send_r.at[k], recv_sem=recv_r.at[k],
            device_id=(w, o ^ 1 << k), device_id_type=MESH,
        )
        relay.start()
        lax.fori_loop(k * blocks // steps, (k + 1) * blocks // steps, near_field, 0)
        relay.wait()

    table = jnp.concatenate([cells[k] for k in range(sets * octs)], axis=0)
    picked = picks[...].reshape(blocks * far, sets * octs).astype(BF)
    chosen = sum(dot(picked, part.astype(BF)) for part in split3(table))
    chosen = chosen * slots[...].reshape(blocks * far, LANES)
    spread = (
        lax.broadcasted_iota(jnp.int32, (LANES, LANES), 0) // blocks
        == lax.broadcasted_iota(jnp.int32, (LANES, LANES), 1)
    ).astype(F32).astype(BF)
    param = sum(dot(part.astype(BF), spread) for part in split3(chosen))

    scale = 1.0 / (near * leaf)
    for b in range(blocks):
        par = param[b * far : (b + 1) * far]
        own = [soa[a, b : b + 1, :] for a in range(3)]
        col = [par[:, k : k + 1] for k in range(CELL)]
        rel = [own[a] - col[1 + a] for a in range(3)]
        dist_sq = rel[0] * rel[0] + rel[1] * rel[1] + rel[2] * rel[2] + FAR_SOFT
        inverse = lax.rsqrt(dist_sq)
        inv_sq = inverse * inverse
        inv_three = inverse * inv_sq
        inv_five = inv_three * inv_sq
        inv_seven = inv_five * inv_sq
        xx, yy, zz, xy, xz, yz = col[4:]
        qr = [
            xx * rel[0] + xy * rel[1] + xz * rel[2],
            xy * rel[0] + yy * rel[1] + yz * rel[2],
            xz * rel[0] + yz * rel[1] + zz * rel[2],
        ]
        rqr = rel[0] * qr[0] + rel[1] * qr[1] + rel[2] * qr[2]
        radial = -col[0] * inv_three - 2.5 * rqr * inv_seven
        live = lane < cnt_ref[b]
        for a in range(3):
            far_sum = jnp.sum(rel[a] * radial + qr[a] * inv_five, axis=0, keepdims=True)
            result = jnp.where(live, (fields[b, a : a + 1, :] + far_sum) * scale, 0.0)
            out_ref[a : a + 1, b * leaf : (b + 1) * leaf] = result


def solution(mesh):
    wide, octs = mesh.shape["wide"], mesh.shape["oct"]

    def on_device(positions, masses, counts, near_list, far_list):
        blocks, near = near_list.shape
        far = far_list.shape[1]
        bodies = positions.shape[1]
        leaf = bodies // blocks
        steps = octs.bit_length() + wide.bit_length() - 2
        sets = wide.bit_length()
        return pl.pallas_call(
            functools.partial(kernel, wide, octs),
            out_shape=jax.ShapeDtypeStruct((3, bodies), F32),
            in_specs=[pl.BlockSpec(memory_space=pltpu.HBM)] * 5,
            out_specs=pl.BlockSpec(memory_space=pltpu.VMEM),
            scratch_shapes=[
                pltpu.SMEM((blocks,), jnp.int32),
                pltpu.SMEM((blocks, near), jnp.int32),
                pltpu.SMEM((blocks, far), jnp.int32),
                pltpu.VMEM((3, bodies), F32),
                pltpu.VMEM((1, bodies), F32),
                pltpu.VMEM((steps + 1, blocks // 2, TILE, leaf), F32),
                pltpu.VMEM((4, blocks, leaf), F32),
                pltpu.VMEM((blocks, 6 * TILE, leaf), BF),
                pltpu.VMEM((blocks, TILE, leaf), F32),
                pltpu.VMEM((sets * octs, 1, LANES), F32),
                pltpu.VMEM((blocks, far, sets * octs), F32),
                pltpu.VMEM((blocks, far, LANES), F32),
                pltpu.VMEM((blocks, TILE, leaf), F32),
                pltpu.SemaphoreType.DMA((5,)),
                pltpu.SemaphoreType.DMA((steps,)),
                pltpu.SemaphoreType.DMA((steps,)),
                pltpu.SemaphoreType.DMA((sets - 1,)),
                pltpu.SemaphoreType.DMA((sets - 1,)),
                pltpu.SemaphoreType.DMA((octs.bit_length() - 1,)),
                pltpu.SemaphoreType.DMA((octs.bit_length() - 1,)),
            ],
            compiler_params=pltpu.CompilerParams(
                collective_id=0, has_side_effects=True, vmem_limit_bytes=32 * 1024 * 1024
            ),
        )(counts, near_list, far_list, positions, masses.reshape(1, bodies))

    return jax.shard_map(
        on_device,
        mesh=mesh,
        in_specs=(
            P(None, ("wide", "oct")),
            P(("wide", "oct")),
            P(("wide", "oct")),
            P(("wide", "oct"), None),
            P(("wide", "oct"), None),
        ),
        out_specs=P(None, ("wide", "oct")),
        check_vma=False,
    )
```

```python
import functools

import jax
import jax.numpy as jnp
from jax import lax
from jax.experimental import pallas as pl
from jax.experimental.pallas import tpu as pltpu
from jax.sharding import PartitionSpec as P

NEAR_SOFT = 0.01
FAR_SOFT = 0.25
MESH = pl.DeviceIdType.MESH
TILE = 8
LANES = 128
CELL = 10
BF = jnp.bfloat16
F32 = jnp.float32
NT = (((1,), (1,)), ((), ()))


def split3(a):
    one = a.astype(BF).astype(F32)
    rest = a - one
    two = rest.astype(BF).astype(F32)
    return one, two, rest - two


def dot(a, b):
    return jnp.dot(a, b, preferred_element_type=F32)


def kernel(
    wide, octs, cnt_in, near_in, far_in, pos_in, mass_in, out_ref,
    cnt_ref, near_ref, far_ref, pos_ref, mass_ref,
    src, soa, feat, centre, cells, picks, slots, fields, load, send_n, recv_n, send_c, recv_c, send_r, recv_r,
):
    blocks, near = near_ref.shape
    far = far_ref.shape[1]
    leaf = pos_ref.shape[1] // blocks
    w, o = lax.axis_index("wide"), lax.axis_index("oct")
    flips = [(0, 1 << k) for k in range(octs.bit_length() - 1)]
    flips += [(1 << k, 0) for k in range(wide.bit_length() - 1)]
    sets = wide.bit_length()
    barrier = pltpu.get_barrier_semaphore()
    greet = flips + [(0, x) for x in range(1, octs) if x & (x - 1)]
    for f, x in greet:
        pl.semaphore_signal(barrier, inc=1, device_id=(w ^ f, o ^ x), device_id_type=MESH)

    taken = [
        pltpu.make_async_copy(a, b, load.at[k])
        for k, (a, b) in enumerate([
            (pos_in, pos_ref), (mass_in, mass_ref), (cnt_in, cnt_ref), (near_in, near_ref), (far_in, far_ref),
        ])
    ]
    for copy in taken:
        copy.start()
    for copy in taken[:3]:
        copy.wait()

    lane = lax.broadcasted_iota(jnp.int32, (1, leaf), 1)
    for b in range(blocks):
        cols = slice(b * leaf, (b + 1) * leaf)
        row = b % 2 * 4
        xyz = pos_ref[:, cols]
        live = jnp.where(lane < cnt_ref[b], mass_ref[:, cols], 0.0)
        src[0, b // 2, row : row + 3, :] = xyz
        src[0, b // 2, row + 3 : row + 4, :] = live
        for a in range(3):
            soa[a, b : b + 1, :] = xyz[a : a + 1]
        soa[3, b : b + 1, :] = live

    pl.semaphore_wait(barrier, len(greet))
    copies = []
    for k, (f, x) in enumerate(flips):
        copies.append(pltpu.make_async_remote_copy(
            src_ref=src.at[0], dst_ref=src.at[k + 1], send_sem=send_n.at[k], recv_sem=recv_n.at[k],
            device_id=(w ^ f, o ^ x), device_id_type=MESH,
        ))
    for copy in copies:
        copy.start()

    mass = soa[3]
    total = jnp.sum(mass, axis=1, keepdims=True)
    mid = [jnp.sum(mass * soa[a], axis=1, keepdims=True) / total for a in range(3)]
    off = [soa[a] - mid[a] for a in range(3)]
    radius_sq = off[0] * off[0] + off[1] * off[1] + off[2] * off[2]
    trace = jnp.sum(mass * radius_sq, axis=1, keepdims=True)

    def second(i, j):
        return jnp.sum(mass * 3.0 * off[i] * off[j], axis=1, keepdims=True)

    moments = [total] + mid
    moments += [second(a, a) - trace for a in range(3)]
    moments += [second(0, 1), second(0, 2), second(1, 2)]
    at = lax.broadcasted_iota(jnp.int32, (blocks, LANES), 1)
    held = jnp.zeros((blocks, LANES), F32)
    for k, moment in enumerate(moments):
        held = jnp.where(at // blocks == k, moment, held)
    held = jnp.where(at % blocks == lax.broadcasted_iota(jnp.int32, (blocks, LANES), 0), held, 0.0)
    cells[0] = jnp.sum(held, axis=0, keepdims=True)

    for k in range(sets - 1):
        copies.append(pltpu.make_async_remote_copy(
            src_ref=cells.at[0], dst_ref=cells.at[k + 1], send_sem=send_c.at[k], recv_sem=recv_c.at[k],
            device_id=(w ^ 1 << k, o), device_id_type=MESH,
        ))
    for copy in copies[len(flips) :]:
        copy.start()

    for copy in taken[3:]:
        copy.wait()
    lane_at = lax.broadcasted_iota(jnp.int32, (1, LANES), 1)
    set_at = lax.broadcasted_iota(jnp.int32, (1, sets * octs), 1)

    def name_cells(b, carry):
        for v in range(far):
            name = far_ref[b, v]
            rest = name % (octs * blocks)
            which = ((rest // blocks) ^ o) * sets + name // (octs * blocks)
            picks[b, v : v + 1, :] = jnp.where(set_at == which, 1.0, 0.0)
            slots[b, v : v + 1, :] = jnp.where(lane_at % blocks == rest % blocks, 1.0, 0.0)
        return carry

    lax.fori_loop(0, blocks, name_cells, 0)

    sub = lax.broadcasted_iota(jnp.int32, (TILE, leaf), 0)
    for b in range(blocks):
        c = [jnp.broadcast_to(mid[a][b : b + 1], (1, leaf)) for a in range(3)]
        rows = jnp.where(sub == 0, c[0], jnp.where(sub == 1, c[1], jnp.where(sub == 2, c[2], 0.0)))
        centre[b] = rows
        p = [off[a][b : b + 1] for a in range(3)]
        norm = radius_sq[b : b + 1] + NEAR_SOFT
        t = jnp.where(sub == 0, p[0], jnp.where(sub == 1, p[1], p[2])) * -2.0
        t = jnp.where(sub < 3, t, jnp.where(sub == 3, 1.0, jnp.where(sub == 4, norm, 0.0)))
        t1, t2, t3 = split3(t)
        stack = jnp.concatenate([t1, t2, t3, t1, t2, t1], axis=0)
        feat[b] = stack.astype(BF)

    for copy in copies:
        copy.wait()

    def near_field(b, carry):
        mid_b = centre[b]
        grid = feat[b]
        acc = jnp.zeros((4 * TILE, leaf), F32)
        for v in range(near):
            name = near_ref[b, v]
            slot = name % blocks
            raw = src[name // blocks, slot // 2]
            raw = jnp.where(slot % 2 == 1, pltpu.roll(raw, 4, 0), raw)
            m = raw[3:4]
            q = jnp.where(sub < 3, raw - mid_b, 0.0)
            norm = jnp.sum(q * q, axis=0, keepdims=True)
            s = jnp.where(sub < 3, q, jnp.where(sub == 3, norm, jnp.where(sub == 4, 1.0, 0.0)))
            s1, s2, s3 = split3(s)
            stack = jnp.concatenate([s1, s1, s1, s2, s2, s3], axis=0).astype(BF)
            a1, a2, a3 = split3(jnp.where(sub < 3, q, jnp.where(sub == 3, 1.0, 0.0)) * m)
            amount = jnp.concatenate([a1, a2, a3, jnp.zeros_like(a1)], axis=0).astype(BF)
            dist_sq = jnp.maximum(lax.dot_general(stack, grid, (((0,),(0,)),((),())), preferred_element_type=F32), NEAR_SOFT)
            inverse = lax.rsqrt(dist_sq)
            weight = inverse * inverse * inverse
            high = weight.astype(BF)
            low = (weight - high.astype(F32)).astype(BF)
            acc += dot(amount, high)
            acc += dot(amount, low)
        acc = acc[:TILE] + acc[TILE : 2 * TILE] + acc[2 * TILE : 3 * TILE]
        pair = src[0, b // 2]
        own = jnp.where(b % 2 == 1, pltpu.roll(pair, 4, 0), pair)
        fields[b, :3, :] = acc[:3] - (own - mid_b)[:3] * acc[3:4]
        return carry

    relays = []
    for x in range(1, octs):
        relays.append(pltpu.make_async_remote_copy(
            src_ref=cells.at[pl.ds(0, sets)], dst_ref=cells.at[pl.ds(x * sets, sets)],
            send_sem=send_r.at[x - 1], recv_sem=recv_r.at[x - 1],
            device_id=(w, o ^ x), device_id_type=MESH,
        ))
    for relay in relays:
        relay.start()
    lax.fori_loop(0, blocks, near_field, 0)
    for relay in relays:
        relay.wait()

    table = jnp.concatenate([cells[k] for k in range(sets * octs)], axis=0)
    picked = picks[...].reshape(blocks * far, sets * octs).astype(BF)
    chosen = sum(dot(picked, part.astype(BF)) for part in split3(table))
    chosen = chosen * slots[...].reshape(blocks * far, LANES)
    spread = (
        lax.broadcasted_iota(jnp.int32, (LANES, LANES), 0) // blocks
        == lax.broadcasted_iota(jnp.int32, (LANES, LANES), 1)
    ).astype(F32).astype(BF)
    param = sum(dot(part.astype(BF), spread) for part in split3(chosen))

    scale = 1.0 / (near * leaf)
    for b in range(blocks):
        par = param[b * far : (b + 1) * far]
        own = [soa[a, b : b + 1, :] for a in range(3)]
        col = [par[:, k : k + 1] for k in range(CELL)]
        rel = [own[a] - col[1 + a] for a in range(3)]
        dist_sq = rel[0] * rel[0] + rel[1] * rel[1] + rel[2] * rel[2] + FAR_SOFT
        inverse = lax.rsqrt(dist_sq)
        inv_sq = inverse * inverse
        inv_three = inverse * inv_sq
        inv_five = inv_three * inv_sq
        inv_seven = inv_five * inv_sq
        xx, yy, zz, xy, xz, yz = col[4:]
        qr = [
            xx * rel[0] + xy * rel[1] + xz * rel[2],
            xy * rel[0] + yy * rel[1] + yz * rel[2],
            xz * rel[0] + yz * rel[1] + zz * rel[2],
        ]
        rqr = rel[0] * qr[0] + rel[1] * qr[1] + rel[2] * qr[2]
        radial = -col[0] * inv_three - 2.5 * rqr * inv_seven
        live = lane < cnt_ref[b]
        for a in range(3):
            far_sum = jnp.sum(rel[a] * radial + qr[a] * inv_five, axis=0, keepdims=True)
            result = jnp.where(live, (fields[b, a : a + 1, :] + far_sum) * scale, 0.0)
            out_ref[a : a + 1, b * leaf : (b + 1) * leaf] = result


def solution(mesh):
    wide, octs = mesh.shape["wide"], mesh.shape["oct"]

    def on_device(positions, masses, counts, near_list, far_list):
        blocks, near = near_list.shape
        far = far_list.shape[1]
        bodies = positions.shape[1]
        leaf = bodies // blocks
        steps = octs.bit_length() + wide.bit_length() - 2
        sets = wide.bit_length()
        return pl.pallas_call(
            functools.partial(kernel, wide, octs),
            out_shape=jax.ShapeDtypeStruct((3, bodies), F32),
            in_specs=[pl.BlockSpec(memory_space=pltpu.HBM)] * 5,
            out_specs=pl.BlockSpec(memory_space=pltpu.VMEM),
            scratch_shapes=[
                pltpu.SMEM((blocks,), jnp.int32),
                pltpu.SMEM((blocks, near), jnp.int32),
                pltpu.SMEM((blocks, far), jnp.int32),
                pltpu.VMEM((3, bodies), F32),
                pltpu.VMEM((1, bodies), F32),
                pltpu.VMEM((steps + 1, blocks // 2, TILE, leaf), F32),
                pltpu.VMEM((4, blocks, leaf), F32),
                pltpu.VMEM((blocks, 6 * TILE, leaf), BF),
                pltpu.VMEM((blocks, TILE, leaf), F32),
                pltpu.VMEM((sets * octs, 1, LANES), F32),
                pltpu.VMEM((blocks, far, sets * octs), F32),
                pltpu.VMEM((blocks, far, LANES), F32),
                pltpu.VMEM((blocks, TILE, leaf), F32),
                pltpu.SemaphoreType.DMA((5,)),
                pltpu.SemaphoreType.DMA((steps,)),
                pltpu.SemaphoreType.DMA((steps,)),
                pltpu.SemaphoreType.DMA((sets - 1,)),
                pltpu.SemaphoreType.DMA((sets - 1,)),
                pltpu.SemaphoreType.DMA((octs - 1,)),
                pltpu.SemaphoreType.DMA((octs - 1,)),
            ],
            compiler_params=pltpu.CompilerParams(
                collective_id=0, has_side_effects=True, vmem_limit_bytes=32 * 1024 * 1024
            ),
        )(counts, near_list, far_list, positions, masses.reshape(1, bodies))

    return jax.shard_map(
        on_device,
        mesh=mesh,
        in_specs=(
            P(None, ("wide", "oct")),
            P(("wide", "oct")),
            P(("wide", "oct")),
            P(("wide", "oct"), None),
            P(("wide", "oct"), None),
        ),
        out_specs=P(None, ("wide", "oct")),
        check_vma=False,
    )
```
